32 devices in a mesh: groups: 2 (over x), dp: 16 (over z, y, core).
Axes of the slice: x: 2, y: 2, z: 4, core: 2. Of those that a mesh axis runs over, the one named last changes fastest.
Arguments:
- activations: bfloat16 [4096, 8192], P(('groups', 'dp')), parts along dimension 0, may hold values from -6 to 6
- upstream: bfloat16 [4096, 1024], P(('groups', 'dp')), parts along dimension 0, may hold values from -6 to 6
- row_job_labels: int32 [4096], P(('groups', 'dp')), parts along dimension 0, may hold values from 0 to 15, as said below
- value_projection_weight: bfloat16 [8192, 1024], P('dp'), may hold values from -0.0625 to 0.0625
- adapter_down_weight: bfloat16 [16, 8192, 64], P('dp'), may hold values from -0.0625 to 0.0625
- adapter_up_weight: bfloat16 [16, 64, 1024], P('dp'), may hold values from -0.75 to 0.75
Outputs:
- projected: bfloat16 [4096, 1024], P(('groups', 'dp')), parts along dimension 0
- entering_derivative: bfloat16 [4096, 8192], P(('groups', 'dp')), parts along dimension 0
- down_grad: float32 [32, 8192, 64], P(('groups', 'dp')), parts along dimension 0
- up_adapter_gradient: float32 [32, 64, 1024], P(('groups', 'dp')), parts along dimension 0
The draws below stay inside these ranges and needn't reach their ends.
There are 2 independent parts, one for each index of `groups`. The reference program is written for one: setup_inputs(seed, part) draws one part's arguments, and reference() takes and returns one part's arrays. A program takes and returns all parts, laid end to end along the dimension named above; an argument that names none is the same for every part. Nothing has to cross between parts.
Inputs may be any that keep to these rules, and one draw needn't show every extreme that they name: `row_job_labels`: in each device's rows the two jobs j and j + 8 together are named at most 2 * 16 times, and on some device exactly so.
All inputs are finite; a program needn't handle non-finite values.
Results may differ from the reference program's by a relative error of at most 0.0055.
Values may be sent and summed in bfloat16 or wider, within the bound.
No kernel may reach another device: no remote copies, remote signals or barrier semaphores. Data moves between devices by JAX's collectives and lax.ppermute only.
A program may use at most 128 MiB of HBM per device.

```python
import jax
import jax.numpy as jnp
from jax import lax

MODEL_WIDTH = 8192
VALUE_FEATURES = 1024
ADAPTER_RANK = 64
TOK_DEV = 128
ADAPTER_JOBS = 16
CAP = 16
TOKENS = 2048
N_DP = 16


def draw_row_job_labels(key, part):
    key = jax.random.fold_in(key, 11)
    stochastic_seed_additional, random_key_drawn, random_key_pinned, random_key_choice = jax.random.split(key, 4)
    companion_tally = ADAPTER_JOBS // 2
    slot_count = ADAPTER_JOBS * CAP
    companion_position = jnp.arange(slot_count, dtype=jnp.int32) // (2 * CAP)
    additional_reward = jax.random.randint(stochastic_seed_additional, (companion_tally,), 0, 4, dtype=jnp.int32)
    baseline_merit = jax.random.randint(random_key_drawn, (ADAPTER_JOBS, slot_count), 0, 4096, dtype=jnp.int32)
    compelled_assignment = jax.random.randint(random_key_pinned, (ADAPTER_JOBS,), 0, companion_tally, dtype=jnp.int32)
    draw_score = baseline_merit + (additional_reward[companion_position] * 2048)[None, :]
    draw_score = draw_score + jnp.where(companion_position[None, :] == compelled_assignment[:, None], 16384, 0).astype(jnp.int32)
    draw_score = draw_score * slot_count + jnp.arange(slot_count, dtype=jnp.int32)[None, :]
    picked_values, picked = lax.top_k(draw_score, TOK_DEV)
    pair_index = picked // (2 * CAP)
    side = jax.random.randint(random_key_choice, (ADAPTER_JOBS, TOK_DEV), 0, 2, dtype=jnp.int32)
    return (pair_index + side * companion_tally).reshape(-1).astype(jnp.int32)


def steps_of(stream_key, dims, pieces, low, largest):
    level, own = 1.0, jax.random.fold_in(stream_key, 6)
    for position, blocks in pieces:
        draws = jnp.exp(jax.random.uniform(jax.random.fold_in(own, position), (blocks,), jnp.float32, low / len(pieces), largest / len(pieces)))
        level = level * jnp.repeat(draws, dims[position] // blocks).reshape([-1 if axis == position else 1 for axis in range(len(dims))])
    return level


def centred(rng, shape, deviation, reach, cuts=(), kind=jnp.bfloat16):
    result = jax.random.normal(rng, shape, jnp.float32) * deviation
    if len(cuts) > 0:
        result = steps_of(rng, shape, cuts, -0.22, 0.18) * result
    return jnp.clip(result, min=-reach, max=reach).astype(kind)


def setup_inputs(seed: int = 0, part: int = 0) -> dict:
    splits = jax.random.split(jax.random.key(seed), 7)
    part_keys = jax.random.split(jax.random.fold_in(splits[6], part), 7)
    activations = centred(part_keys[0], (TOKENS, MODEL_WIDTH), 1.0, 6.0, ((0, 16),))
    upstream = centred(part_keys[1], (TOKENS, VALUE_FEATURES), 1.0, 6.0, ((0, 16),))
    row_job_labels = draw_row_job_labels(jax.random.fold_in(jax.random.fold_in(splits[6], part), 71), part)
    value_projection_weight = centred(splits[3], (MODEL_WIDTH, VALUE_FEATURES), MODEL_WIDTH ** -0.5, 0.0625, ((0, 16),))
    adapter_down_weight = centred(splits[4], (ADAPTER_JOBS, MODEL_WIDTH, ADAPTER_RANK), MODEL_WIDTH ** -0.5, 0.0625, ((0, 16),))
    adapter_up_weight = centred(splits[5], (ADAPTER_JOBS, ADAPTER_RANK, VALUE_FEATURES), ADAPTER_RANK ** -0.5, 0.75, ((0, 16),))
    return dict(activations=activations, upstream=upstream, row_job_labels=row_job_labels, value_projection_weight=value_projection_weight, adapter_down_weight=adapter_down_weight, adapter_up_weight=adapter_up_weight)


ADAPTER_SCALE = 2.0


def reference(activations, upstream, row_job_labels, value_projection_weight, adapter_down_weight, adapter_up_weight):
    frozen_output = jnp.dot(activations, value_projection_weight, preferred_element_type=jnp.float32)
    frozen_backward = jnp.dot(upstream, value_projection_weight.T, preferred_element_type=jnp.float32)
    sort_permutation = jnp.argsort(row_job_labels, stable=True).astype(jnp.int32)
    sorted_rows = activations[sort_permutation]
    sorted_grads = upstream[sort_permutation]
    job_range = jnp.arange(ADAPTER_JOBS, dtype=jnp.int32)
    counts = jnp.sum((row_job_labels[:, None] == job_range[None, :]).astype(jnp.int32), axis=0)
    offsets = (jnp.cumsum(counts) - counts).astype(jnp.int32)
    window = min(TOKENS, 2 * N_DP * CAP)
    window_iota = jnp.arange(window, dtype=jnp.int32)
    zero_value = jnp.zeros((), activations.dtype)

    def per_job(carry, current_job_index):
        output_rows, backward_rows = carry
        first = offsets[current_job_index]
        start_offset = jnp.minimum(first, TOKENS - window).astype(jnp.int32)
        index_rows = start_offset + window_iota
        inside = (index_rows >= first) & (index_rows < first + counts[current_job_index])
        rows_in = jnp.where(inside[:, None], lax.dynamic_slice_in_dim(sorted_rows, start_offset, window, 0), zero_value)
        incoming_gradient = jnp.where(inside[:, None], lax.dynamic_slice_in_dim(sorted_grads, start_offset, window, 0), zero_value)
        down_adapter = adapter_down_weight[current_job_index]
        upper_limit = adapter_up_weight[current_job_index]
        summed_result = jnp.dot(rows_in, down_adapter, preferred_element_type=jnp.float32).astype(activations.dtype)
        adapter_output = (ADAPTER_SCALE * jnp.dot(summed_result, upper_limit, preferred_element_type=jnp.float32)).astype(activations.dtype)
        scaled_output = (ADAPTER_SCALE * jnp.dot(incoming_gradient, upper_limit.T, preferred_element_type=jnp.float32)).astype(activations.dtype)
        adapter_backward = jnp.dot(scaled_output, down_adapter.T, preferred_element_type=jnp.float32).astype(activations.dtype)
        down_part = jnp.dot(rows_in.T, scaled_output, preferred_element_type=jnp.float32)
        partial_up_adapter = ADAPTER_SCALE * jnp.dot(summed_result.T, incoming_gradient, preferred_element_type=jnp.float32)
        prior_output = lax.dynamic_slice_in_dim(output_rows, start_offset, window, 0)
        output_rows = lax.dynamic_update_slice_in_dim(output_rows, prior_output + adapter_output.astype(jnp.float32), start_offset, 0)
        prior_backward = lax.dynamic_slice_in_dim(backward_rows, start_offset, window, 0)
        backward_rows = lax.dynamic_update_slice_in_dim(backward_rows, prior_backward + adapter_backward.astype(jnp.float32), start_offset, 0)
        return (output_rows, backward_rows), (down_part, partial_up_adapter)

    start_carry = (jnp.zeros((TOKENS, VALUE_FEATURES), jnp.float32), jnp.zeros((TOKENS, MODEL_WIDTH), jnp.float32))
    (output_rows, backward_rows), (down_grad, up_adapter_gradient) = lax.scan(per_job, start_carry, job_range)
    adapter_output_full = jnp.zeros_like(output_rows).at[sort_permutation].set(output_rows)
    adapter_backward_full = jnp.zeros_like(backward_rows).at[sort_permutation].set(backward_rows)
    projected = (frozen_output + adapter_output_full).astype(activations.dtype)
    entering_derivative = (frozen_backward + adapter_backward_full).astype(activations.dtype)
    return projected, entering_derivative, down_grad, up_adapter_gradient
```

```python
import functools

import jax
import jax.numpy as jnp
from jax import lax
from jax.sharding import Mesh
from jax.sharding import PartitionSpec as P

ADAPTER_SCALE = 2.0
PLANE = ("groups", "q")
F32 = jnp.float32
BF16 = jnp.bfloat16


def swapped(array, axis, bit):
    peers = lax.axis_size(axis)
    return lax.ppermute(array, axis, [(i, i ^ bit) for i in range(peers)])


def shifted(array, axis, by):
    peers = lax.axis_size(axis)
    return lax.ppermute(array, axis, [(i, (i + by) % peers) for i in range(peers)])


def cube_gather(array, axes):
    stack = array[None]
    for axis in axes:
        bit = lax.axis_size(axis) // 2
        while bit:
            mine = (lax.axis_index(axis) & bit) > 0
            other = swapped(stack, axis, bit)
            pair = jnp.stack(
                [jnp.where(mine, other, stack), jnp.where(mine, stack, other)], axis=1
            )
            stack = pair.reshape((-1,) + array.shape)
            bit //= 2
    return stack


def straight_gather(array, axis):
    peers = lax.axis_size(axis)
    me = lax.axis_index(axis)
    stack = jnp.zeros((peers,) + array.shape, array.dtype)
    stack = lax.dynamic_update_index_in_dim(stack, array, me, 0)
    for by in range(1, peers):
        got = shifted(array, axis, by)
        stack = lax.dynamic_update_index_in_dim(stack, got, (me - by) % peers, 0)
    return stack


def line_gather(array, axis):
    peers = lax.axis_size(axis)
    me = lax.axis_index(axis)
    upward = [(i, i + 1) for i in range(peers - 1)]
    downward = [(i + 1, i) for i in range(peers - 1)]
    rising, falling = [array], [array]
    for _ in range(peers - 1):
        rising.append(lax.ppermute(rising[-1], axis, upward))
        falling.append(lax.ppermute(falling[-1], axis, downward))
    stack = jnp.zeros((peers,) + array.shape, array.dtype)
    stack = lax.dynamic_update_index_in_dim(stack, array, me, 0)
    for by in range(1, peers):
        block = jnp.where(me >= by, rising[by], falling[peers - by])
        stack = lax.dynamic_update_index_in_dim(stack, block, (me - by) % peers, 0)
    return stack


def exchanged(array, axes):
    return lax.all_to_all(array, axes, split_axis=0, concat_axis=0, tiled=True)


def dot(left, right, left_dim, right_dim):
    return lax.dot_general(
        left, right, (((left_dim,), (right_dim,)), ((), ())), preferred_element_type=F32
    )


def per_device(
    activations,
    upstream,
    row_job_labels,
    value_projection_weight,
    adapter_down_weight,
    adapter_up_weight,
):
    rows, width = activations.shape
    out_width = upstream.shape[1]
    rank = adapter_down_weight.shape[2]
    groups, outer, inner = (lax.axis_size(a) for a in ("groups", "z", "q"))
    group, level, place = (lax.axis_index(a) for a in ("groups", "z", "q"))
    plane = groups * inner
    jobs = outer * inner
    piece = width // (jobs * groups)
    flat = outer * piece
    plane_rows = plane * rows

    def spread(values, labels, first, count):
        wanted = first + jnp.arange(count, dtype=jnp.int32)
        hit = labels[None, None, :] == wanted[:, None, None]
        wide = jnp.where(hit, values[None], jnp.zeros((), values.dtype))
        return wide.reshape(count * rank, -1)

    def gathered_in(wide, labels, order):
        hit = labels[None, None, :] == order[:, None, None]
        return jnp.sum(jnp.where(hit, wide.reshape(order.shape[0], rank, -1), 0.0), axis=0)

    up_line = straight_gather(adapter_up_weight[0], "z")
    up_all = cube_gather(up_line.reshape(outer * rank, out_width), ("q",))
    up_all = up_all.reshape(jobs * rank, out_width)
    up_order = (
        jnp.arange(outer, dtype=jnp.int32)[None, :] * inner
        + jnp.arange(inner, dtype=jnp.int32)[:, None]
    ).reshape(-1)

    act_send = activations.reshape(rows, outer, inner, groups, piece)
    act_send = act_send.transpose(3, 2, 0, 1, 4).reshape(plane_rows, flat)
    act_plane = exchanged(act_send, PLANE)
    act_deep = act_plane.reshape(plane_rows, outer, piece).transpose(1, 0, 2)
    act_deep = exchanged(act_deep.reshape(outer * plane_rows, piece), "z")

    part = value_projection_weight.shape[0] // groups
    weight_half = lax.dynamic_slice_in_dim(value_projection_weight, group * part, part, 0)
    weight = line_gather(weight_half, "z").reshape(flat, out_width)
    down_send = adapter_down_weight[0].T.reshape(rank, outer, inner, groups, piece)
    down_send = lax.dynamic_index_in_dim(down_send, group, 3, keepdims=False)
    down_send = down_send.transpose(2, 0, 1, 3).reshape(inner * rank, flat)
    down_block = exchanged(down_send, "q")
    down = line_gather(down_block, "z")

    labels_plane = cube_gather(row_job_labels, PLANE)
    labels_deep = straight_gather(labels_plane, "z")
    labels_plane = labels_plane.reshape(-1)
    upstream_plane = cube_gather(upstream, PLANE)

    wide = ADAPTER_SCALE * dot(up_all, upstream, 1, 1)
    scaled = gathered_in(wide, row_job_labels, up_order).astype(BF16)
    scaled_plane = cube_gather(scaled, PLANE)
    scaled_deep = straight_gather(scaled_plane, "z")
    scaled_plane = scaled_plane.transpose(1, 0, 2).reshape(rank, plane_rows)

    act_deep = act_deep.reshape(outer, groups, inner * rows, piece)
    scaled_deep = scaled_deep.reshape(outer, groups, inner, rank, rows)
    scaled_deep = scaled_deep.transpose(1, 3, 0, 2, 4).reshape(groups, rank, -1)
    labels_deep = labels_deep.reshape(outer, groups, inner * rows)
    small = jobs * rank * outer * inner * rows <= 1 << 22

    def down_grad_part(g, first, count):
        columns = act_deep[:, g].reshape(-1, piece)
        wide = spread(scaled_deep[g], labels_deep[:, g].reshape(-1), first, count)
        return dot(wide, columns, 1, 0).astype(BF16)

    if small:
        down_parts = [down_grad_part(g, 0, jobs) for g in range(groups)]
    else:
        down_parts = [
            lax.map(
                functools.partial(lambda g, b: down_grad_part(g, b * inner, inner), g),
                jnp.arange(outer, dtype=jnp.int32),
            ).reshape(jobs * rank, piece)
            for g in range(groups)
        ]
    down_parts = exchanged(jnp.concatenate(down_parts, axis=0), ("groups", "z", "q"))
    down_parts = down_parts.reshape(groups, outer, inner, rank, piece)
    down_grad = down_parts.transpose(3, 1, 2, 0, 4).reshape(rank, width).astype(F32).T

    frozen = dot(act_plane, weight, 1, 0).astype(BF16)
    frozen = exchanged(frozen, PLANE).reshape(plane, rows, out_width)
    frozen = jnp.sum(frozen.astype(F32), axis=0)

    back = dot(upstream_plane.reshape(plane_rows, out_width), weight, 1, 1)
    if small:
        down_all = down.reshape(jobs * rank, flat)
        back = back + dot(spread(scaled_plane, labels_plane, 0, jobs), down_all, 0, 0)
        reduced = gathered_in(
            dot(down_all, act_plane, 1, 1), labels_plane, jnp.arange(jobs, dtype=jnp.int32)
        )
    else:

        def step(carry, operands):
            back, reduced = carry
            block, first = operands
            wide = spread(scaled_plane, labels_plane, first, inner)
            order = first + jnp.arange(inner, dtype=jnp.int32)
            back = back + dot(wide, block, 0, 0)
            reduced = reduced + gathered_in(dot(block, act_plane, 1, 1), labels_plane, order)
            return (back, reduced), None

        firsts = jnp.arange(outer, dtype=jnp.int32) * inner
        start = (back, jnp.zeros((rank, plane_rows), F32))
        (back, reduced), _ = lax.scan(step, start, (down, firsts))
    back = exchanged(back.astype(BF16), PLANE)
    entering_derivative = back.reshape(groups, inner, rows, outer, piece)
    entering_derivative = entering_derivative.transpose(2, 3, 1, 0, 4).reshape(rows, width)

    reduced = reduced.reshape(rank, groups, inner * rows)
    total = lax.dynamic_index_in_dim(reduced, group, 1, keepdims=False)
    for by in range(1, groups):
        leaving = lax.dynamic_index_in_dim(reduced, (group + by) % groups, 1, keepdims=False)
        total = total + shifted(leaving, "groups", by)
    bit = inner // 2
    while bit:
        total = total + swapped(total, "q", bit)
        bit //= 2
    reduced = total.astype(BF16)
    reduced_own = lax.dynamic_slice_in_dim(reduced, place * rows, rows, 1)

    hit = row_job_labels[None, None, :] == up_order[:, None, None]
    wide = jnp.where(hit, reduced_own[None], jnp.zeros((), BF16)).reshape(jobs * rank, rows)
    projected = (frozen + ADAPTER_SCALE * dot(wide, up_all, 0, 0)).astype(BF16)

    upstream_group = lax.dynamic_index_in_dim(
        upstream_plane.reshape(groups, inner * rows, out_width), group, 0, keepdims=False
    )
    labels_group = lax.dynamic_index_in_dim(
        labels_plane.reshape(groups, inner * rows), group, 0, keepdims=False
    )
    wanted = jnp.arange(outer, dtype=jnp.int32) * inner + place
    hit = labels_group[None, None, :] == wanted[:, None, None]
    wide = jnp.where(hit, reduced[None], jnp.zeros((), BF16)).reshape(outer * rank, -1)
    up_part = (ADAPTER_SCALE * dot(wide, upstream_group, 1, 0)).reshape(outer, rank, out_width)
    up_grad = lax.dynamic_index_in_dim(up_part, level, 0, keepdims=False)
    up_send = up_part.astype(BF16)
    for by in range(1, outer):
        leaving = lax.dynamic_index_in_dim(up_send, (level + by) % outer, 0, keepdims=False)
        up_grad = up_grad + shifted(leaving, "z", by).astype(F32)
    return (projected, entering_derivative, down_grad[None], up_grad[None])


def solution(mesh):
    groups, devices = mesh.devices.shape
    inner = 1
    while inner * inner < devices:
        inner *= 2
    fine = Mesh(
        mesh.devices.reshape(groups, devices // inner, inner), ("groups", "z", "q")
    )
    every = ("groups", "z", "q")
    owner = ("z", "q")
    return jax.shard_map(
        per_device,
        mesh=fine,
        in_specs=(
            P(every, None),
            P(every, None),
            P(every),
            P(owner, None),
            P(owner, None, None),
            P(owner, None, None),
        ),
        out_specs=(
            P(every, None),
            P(every, None),
            P(every, None, None),
            P(every, None, None),
        ),
        check_vma=False,
    )
```

```python
import functools

import jax
import jax.numpy as jnp
from jax import lax
from jax.experimental import pallas as pl
from jax.experimental.pallas import tpu as pltpu
from jax.sharding import Mesh
from jax.sharding import PartitionSpec as P

ADAPTER_SCALE = 2.0
PLANE = ("groups", "q")
F32 = jnp.float32
BF16 = jnp.bfloat16


def swapped(array, axis, bit):
    peers = lax.axis_size(axis)
    return lax.ppermute(array, axis, [(i, i ^ bit) for i in range(peers)])


def shifted(array, axis, by):
    peers = lax.axis_size(axis)
    return lax.ppermute(array, axis, [(i, (i + by) % peers) for i in range(peers)])


def cube_gather(array, axes):
    stack = array[None]
    for axis in axes:
        bit = lax.axis_size(axis) // 2
        while bit:
            mine = (lax.axis_index(axis) & bit) > 0
            other = swapped(stack, axis, bit)
            pair = jnp.stack(
                [jnp.where(mine, other, stack), jnp.where(mine, stack, other)], axis=1
            )
            stack = pair.reshape((-1,) + array.shape)
            bit //= 2
    return stack


def relative(array, axis):
    return [array] + [shifted(array, axis, by) for by in range(1, lax.axis_size(axis))]


def line_gather(array, axis):
    peers = lax.axis_size(axis)
    me = lax.axis_index(axis)
    upward = [(i, i + 1) for i in range(peers - 1)]
    downward = [(i + 1, i) for i in range(peers - 1)]
    rising, falling = [array], [array]
    for _ in range(peers - 1):
        rising.append(lax.ppermute(rising[-1], axis, upward))
        falling.append(lax.ppermute(falling[-1], axis, downward))
    stack = jnp.zeros((peers,) + array.shape, array.dtype)
    stack = lax.dynamic_update_index_in_dim(stack, array, me, 0)
    for by in range(1, peers):
        block = jnp.where(me >= by, rising[by], falling[peers - by])
        stack = lax.dynamic_update_index_in_dim(stack, block, (me - by) % peers, 0)
    return stack


def repacked(array, shape, moves):
    def kernel(source, target):
        for (r, c), (to_r, to_c), (high, wide) in moves:
            target[pl.ds(to_r, high), pl.ds(to_c, wide)] = source[pl.ds(r, high), pl.ds(c, wide)]

    return pl.pallas_call(
        kernel,
        out_shape=jax.ShapeDtypeStruct(shape, array.dtype),
        in_specs=[pl.BlockSpec(memory_space=pltpu.VMEM)],
        out_specs=pl.BlockSpec(memory_space=pltpu.VMEM),
        compiler_params=pltpu.CompilerParams(vmem_limit_bytes=16 << 20),
        cost_estimate=pl.CostEstimate(
            flops=0, bytes_accessed=2 * array.size * array.dtype.itemsize, transcendentals=0
        ),
    )(array)


def exchanged(array, axes):
    return lax.all_to_all(array, axes, split_axis=0, concat_axis=0, tiled=True)


def dot(left, right, left_dim, right_dim):
    return lax.dot_general(
        left, right, (((left_dim,), (right_dim,)), ((), ())), preferred_element_type=F32
    )


def per_device(
    activations,
    upstream,
    row_job_labels,
    value_projection_weight,
    adapter_down_weight,
    adapter_up_weight,
):
    rows, width = activations.shape
    out_width = upstream.shape[1]
    rank = adapter_down_weight.shape[2]
    groups, outer, inner = (lax.axis_size(a) for a in ("groups", "z", "q"))
    group, level, place = (lax.axis_index(a) for a in ("groups", "z", "q"))
    plane = groups * inner
    jobs = outer * inner
    piece = width // (jobs * groups)
    flat = outer * piece
    plane_rows = plane * rows

    def spread(values, labels, first, count):
        wanted = first + jnp.arange(count, dtype=jnp.int32)
        hit = labels[None, None, :] == wanted[:, None, None]
        wide = jnp.where(hit, values[None], jnp.zeros((), values.dtype))
        return wide.reshape(count * rank, -1)

    def own_of(wide, labels, first, count):
        wanted = first + jnp.arange(count, dtype=jnp.int32)
        hit = labels[None, None, :] == wanted[:, None, None]
        return jnp.sum(jnp.where(hit, wide.reshape(count, rank, -1), 0.0), axis=0)

    aligned = piece % 128 == 0 and rows % 16 == 0
    moves = []
    for g in range(groups):
        for p in range(inner):
            for o in range(outer):
                wide_at = (0, ((o * inner + p) * groups + g) * piece)
                flat_at = ((g * inner + p) * rows, o * piece)
                moves.append((wide_at, flat_at, (rows, piece)))

    if aligned:
        act_send = repacked(activations, (plane_rows, flat), moves)
    else:
        act_send = activations.reshape(rows, outer, inner, groups, piece)
        act_send = act_send.transpose(3, 2, 0, 1, 4).reshape(plane_rows, flat)
    act_send, value_projection_weight, adapter_down_weight, upstream, adapter_up_weight = (
        lax.optimization_barrier(
            (act_send, value_projection_weight, adapter_down_weight, upstream, adapter_up_weight)
        )
    )
    act_plane = exchanged(act_send, PLANE)

    part = value_projection_weight.shape[0] // groups
    weight_half = lax.dynamic_slice_in_dim(value_projection_weight, group * part, part, 0)
    weight = line_gather(weight_half, "z").reshape(flat, out_width)
    down_send = adapter_down_weight[0].T.reshape(rank, outer, inner, groups, piece)
    down_send = lax.dynamic_index_in_dim(down_send, group, 3, keepdims=False)
    down_send = down_send.transpose(2, 0, 1, 3).reshape(inner * rank, flat)
    down_block = exchanged(down_send, "q")
    down = line_gather(down_block, "z")

    up_all = lax.all_gather(adapter_up_weight[0], ("z", "q"), axis=0, tiled=True)
    upstream_plane = lax.all_gather(upstream, PLANE, axis=0, tiled=True)

    wide = ADAPTER_SCALE * dot(up_all, upstream, 1, 1)
    scaled = own_of(wide, row_job_labels, 0, jobs).astype(BF16)
    label_rows = jnp.broadcast_to(row_job_labels.astype(BF16)[None], (16, rows))
    packet = cube_gather(jnp.concatenate([scaled, label_rows], axis=0), PLANE)
    packet = packet.transpose(1, 0, 2).reshape(rank + 16, plane_rows)
    packets = relative(packet, "z")
    scaled_plane = packet[:rank]
    labels_plane = packet[rank].astype(jnp.int32)

    blocks = []
    for by in range(outer):
        at = (level + by) % outer * piece
        block = lax.dynamic_slice_in_dim(act_plane, at, piece, 1)
        blocks.append(shifted(block, "z", by) if by else block)

    small = jobs * rank * outer * inner * rows <= 1 << 22
    half = inner * rows

    def down_grad_part(g, first, count):
        total = jnp.zeros((count * rank, piece), F32)
        for packet, block in zip(packets, blocks):
            packet = packet[:, g * half : (g + 1) * half]
            wide = spread(packet[:rank], packet[rank].astype(jnp.int32), first, count)
            total = total + dot(wide, block[g * half : (g + 1) * half], 1, 0)
        return total.astype(BF16)

    if small:
        down_parts = [down_grad_part(g, 0, jobs) for g in range(groups)]
    else:
        down_parts = [
            lax.map(
                functools.partial(lambda g, b: down_grad_part(g, b * inner, inner), g),
                jnp.arange(outer, dtype=jnp.int32),
            ).reshape(jobs * rank, piece)
            for g in range(groups)
        ]
    down_parts = exchanged(jnp.concatenate(down_parts, axis=0), ("groups", "z", "q"))
    down_parts = down_parts.reshape(groups, outer, inner, rank, piece)
    down_grad = down_parts.transpose(3, 1, 2, 0, 4).reshape(rank, width).astype(F32).T

    frozen = dot(act_plane, weight, 1, 0).reshape(groups, inner, rows, out_width)
    bit = 1
    while bit < inner:
        pairs = frozen.reshape(groups, inner // bit // 2, 2, rows, out_width)
        mine = (place // bit) % 2
        kept = lax.dynamic_index_in_dim(pairs, mine, 2, keepdims=False)
        leaving = lax.dynamic_index_in_dim(pairs, 1 - mine, 2, keepdims=False)
        frozen = kept + swapped(leaving.astype(BF16), "q", bit).astype(F32)
        bit *= 2
    frozen = frozen.reshape(groups, rows, out_width)
    total = lax.dynamic_index_in_dim(frozen, group, 0, keepdims=False)
    for by in range(1, groups):
        leaving = lax.dynamic_index_in_dim(frozen, (group + by) % groups, 0, keepdims=False)
        total = total + shifted(leaving.astype(BF16), "groups", by).astype(F32)
    frozen = total

    back = dot(upstream_plane, weight, 1, 1)
    if small:
        down_all = down.reshape(jobs * rank, flat)
        back = back + dot(spread(scaled_plane, labels_plane, 0, jobs), down_all, 0, 0)
        reduced = own_of(dot(down_all, act_plane, 1, 1), labels_plane, 0, jobs)
    else:

        def step(carry, operands):
            back, reduced = carry
            block, first = operands
            back = back + dot(spread(scaled_plane, labels_plane, first, inner), block, 0, 0)
            reduced = reduced + own_of(dot(block, act_plane, 1, 1), labels_plane, first, inner)
            return (back, reduced), None

        firsts = jnp.arange(outer, dtype=jnp.int32) * inner
        start = (back, jnp.zeros((rank, plane_rows), F32))
        (back, reduced), _ = lax.scan(step, start, (down, firsts))
    back = exchanged(back.astype(BF16), PLANE)
    if aligned:
        turned = [(to, at, size) for at, to, size in moves]
        entering_derivative = repacked(back, (rows, width), turned)
    else:
        entering_derivative = back.reshape(groups, inner, rows, outer, piece)
        entering_derivative = entering_derivative.transpose(2, 3, 1, 0, 4).reshape(rows, width)

    reduced = reduced.reshape(rank, groups, inner * rows)
    total = lax.dynamic_index_in_dim(reduced, group, 1, keepdims=False)
    for by in range(1, groups):
        leaving = lax.dynamic_index_in_dim(reduced, (group + by) % groups, 1, keepdims=False)
        total = total + shifted(leaving, "groups", by)
    bit = inner // 2
    while bit:
        total = total + swapped(total, "q", bit)
        bit //= 2
    reduced = total.astype(BF16)
    reduced_own = lax.dynamic_slice_in_dim(reduced, place * rows, rows, 1)

    wide = spread(reduced_own, row_job_labels, 0, jobs)
    projected = (frozen + ADAPTER_SCALE * dot(wide, up_all, 0, 0)).astype(BF16)

    upstream_group = lax.dynamic_slice_in_dim(upstream_plane, group * half, half, 0)
    labels_group = lax.dynamic_slice_in_dim(labels_plane, group * half, half, 0)
    wanted = jnp.arange(outer, dtype=jnp.int32) * inner + place
    hit = labels_group[None, None, :] == wanted[:, None, None]
    wide = jnp.where(hit, reduced[None], jnp.zeros((), BF16)).reshape(outer * rank, -1)
    up_part = (ADAPTER_SCALE * dot(wide, upstream_group, 1, 0)).reshape(outer, rank, out_width)
    up_grad = lax.dynamic_index_in_dim(up_part, level, 0, keepdims=False)
    up_send = up_part.astype(BF16)
    for by in range(1, outer):
        leaving = lax.dynamic_index_in_dim(up_send, (level + by) % outer, 0, keepdims=False)
        up_grad = up_grad + shifted(leaving, "z", by).astype(F32)
    return (projected, entering_derivative, down_grad[None], up_grad[None])


def solution(mesh):
    groups, devices = mesh.devices.shape
    inner = 1
    while inner * inner < devices:
        inner *= 2
    fine = Mesh(
        mesh.devices.reshape(groups, devices // inner, inner), ("groups", "z", "q")
    )
    every = ("groups", "z", "q")
    owner = ("z", "q")
    return jax.shard_map(
        per_device,
        mesh=fine,
        in_specs=(
            P(every, None),
            P(every, None),
            P(every),
            P(owner, None),
            P(owner, None, None),
            P(owner, None, None),
        ),
        out_specs=(
            P(every, None),
            P(every, None),
            P(every, None, None),
            P(every, None, None),
        ),
        check_vma=False,
    )
```

```python
import functools

import jax
import jax.numpy as jnp
import numpy as np
from jax import lax
from jax.experimental import pallas as pl
from jax.experimental.pallas import tpu as pltpu
from jax.sharding import Mesh
from jax.sharding import PartitionSpec as P

ADAPTER_SCALE = 2.0
PLANE = ("groups", "q")
F32 = jnp.float32
BF16 = jnp.bfloat16


def swapped(array, axis, bit):
    peers = lax.axis_size(axis)
    return lax.ppermute(array, axis, [(i, i ^ bit) for i in range(peers)])


def shifted(array, axis, by):
    peers = lax.axis_size(axis)
    return lax.ppermute(array, axis, [(i, (i + by) % peers) for i in range(peers)])


def cube_gather(array, axes):
    stack = array[None]
    for axis in axes:
        bit = lax.axis_size(axis) // 2
        while bit:
            mine = (lax.axis_index(axis) & bit) > 0
            other = swapped(stack, axis, bit)
            pair = jnp.stack(
                [jnp.where(mine, other, stack), jnp.where(mine, stack, other)], axis=1
            )
            stack = pair.reshape((-1,) + array.shape)
            bit //= 2
    return stack


def relative(array, axis):
    return [array] + [shifted(array, axis, by) for by in range(1, lax.axis_size(axis))]


def placed(blocks, axis):
    me = lax.axis_index(axis)
    stack = jnp.zeros((len(blocks),) + blocks[0].shape, blocks[0].dtype)
    for by, block in enumerate(blocks):
        stack = lax.dynamic_update_index_in_dim(stack, block, (me - by) % len(blocks), 0)
    return stack


def repacked(array, shape, moves):
    def kernel(source, target):
        for (r, c), (to_r, to_c), (high, wide) in moves:
            target[pl.ds(to_r, high), pl.ds(to_c, wide)] = source[pl.ds(r, high), pl.ds(c, wide)]

    return pl.pallas_call(
        kernel,
        out_shape=jax.ShapeDtypeStruct(shape, array.dtype),
        in_specs=[pl.BlockSpec(memory_space=pltpu.VMEM)],
        out_specs=pl.BlockSpec(memory_space=pltpu.VMEM),
        compiler_params=pltpu.CompilerParams(vmem_limit_bytes=16 << 20),
        cost_estimate=pl.CostEstimate(
            flops=0, bytes_accessed=2 * array.size * array.dtype.itemsize, transcendentals=0
        ),
    )(array)


def exchanged(array, axes):
    return lax.all_to_all(array, axes, split_axis=0, concat_axis=0, tiled=True)


def dot(left, right, left_dim, right_dim):
    return lax.dot_general(
        left, right, (((left_dim,), (right_dim,)), ((), ())), preferred_element_type=F32
    )


def per_device(
    activations,
    upstream,
    row_job_labels,
    value_projection_weight,
    adapter_down_weight,
    adapter_up_weight,
):
    rows, width = activations.shape
    out_width = upstream.shape[1]
    rank = adapter_down_weight.shape[2]
    groups, outer, inner = (lax.axis_size(a) for a in ("groups", "z", "q"))
    group, level, place = (lax.axis_index(a) for a in ("groups", "z", "q"))
    plane = groups * inner
    jobs = outer * inner
    piece = width // (jobs * groups)
    flat = outer * piece
    plane_rows = plane * rows

    def spread(values, keys, wanted):
        hit = keys[None, None, :] == wanted.astype(np.int32)[:, None, None]
        wide = jnp.where(hit, values[None], jnp.zeros((), values.dtype))
        return wide.reshape(wanted.shape[0] * rank, -1)

    def own_of(wide, keys, wanted):
        hit = keys[None, None, :] == wanted.astype(np.int32)[:, None, None]
        wide = wide.reshape(wanted.shape[0], rank, -1)
        return jnp.sum(jnp.where(hit, wide, 0.0), axis=0)

    aligned = piece % 128 == 0 and rows % 16 == 0
    moves = []
    for g in range(groups):
        for p in range(inner):
            for o in range(outer):
                wide_at = (0, ((o * inner + p) * groups + g) * piece)
                flat_at = ((g * inner + p) * rows, o * piece)
                moves.append((wide_at, flat_at, (rows, piece)))

    if aligned:
        act_send = repacked(activations, (plane_rows, flat), moves)
    else:
        act_send = activations.reshape(rows, outer, inner, groups, piece)
        act_send = act_send.transpose(3, 2, 0, 1, 4).reshape(plane_rows, flat)
    part = value_projection_weight.shape[0] // groups
    weight_half = lax.dynamic_slice_in_dim(value_projection_weight, group * part, part, 0)
    down_send = adapter_down_weight[0].T.reshape(rank, outer, inner, groups, piece)
    down_send = lax.dynamic_index_in_dim(down_send, group, 3, keepdims=False)
    down_send = down_send.transpose(2, 0, 1, 3).reshape(inner, rank, flat)
    down_block = []
    for other in range(inner):
        leaving = lax.dynamic_index_in_dim(down_send, place ^ other, 0, keepdims=False)
        down_block.append(swapped(leaving, "q", other) if other else leaving)
    down_block = jnp.concatenate(down_block, axis=0).reshape(-1, out_width)

    both = jnp.concatenate([weight_half, down_block], axis=0)

    up_own, *up_others = relative(adapter_up_weight[0], "z")
    both, act_send, *up_others = lax.optimization_barrier((both, act_send, *up_others))
    up_all = placed([up_own, *up_others], "z").reshape(1, outer * rank, out_width)
    up_other = swapped(up_all, "q", inner // 2)
    up_jobs = (np.arange(outer)[None, :] * inner + np.arange(inner)[:, None]).reshape(-1)
    act_plane = exchanged(act_send, PLANE)

    shares = {0: (weight_half, down_block)}
    rising, falling = shifted(both, "z", by=1), shifted(both, "z", by=-1)
    act_plane, rising, falling, upstream, up_other = lax.optimization_barrier(
        (act_plane, rising, falling, upstream, up_other)
    )
    for by in range(1, outer // 2):
        if by > 1:
            rising, falling = shifted(rising, "z", by=1), shifted(falling, "z", by=-1)
        shares[by] = rising[:part], rising[part:]
        shares[outer - by] = falling[:part], falling[part:]
    shares[outer // 2] = shifted(rising[:part], "z", by=1), shifted(falling[part:], "z", by=-1)

    bit = inner // 2
    while bit:
        mine = (place & bit) > 0
        other = up_other if bit == inner // 2 else swapped(up_all, "q", bit)
        pair = [jnp.where(mine, other, up_all), jnp.where(mine, up_all, other)]
        up_all = jnp.stack(pair, axis=1).reshape(-1, outer * rank, out_width)
        bit //= 2
    up_all = up_all.reshape(jobs * rank, out_width)

    wide = ADAPTER_SCALE * dot(up_all, upstream, 1, 1)
    scaled = own_of(wide, row_job_labels, up_jobs).astype(BF16)
    label_rows = jnp.broadcast_to(row_job_labels.astype(BF16)[None], (16, rows))
    packet = jnp.concatenate([scaled, label_rows], axis=0)
    act_plane, packet, upstream = lax.optimization_barrier((act_plane, packet, upstream))
    packets = jnp.stack(relative(packet, "z"))

    weight = placed([shares[by][0] for by in range(outer)], "z").reshape(flat, out_width)
    down_all = jnp.concatenate([shares[by][1] for by in range(outer)], axis=0)
    down_all = down_all.reshape(jobs * rank, flat)

    upstream_plane = cube_gather(upstream, PLANE).reshape(plane_rows, out_width)
    packets = cube_gather(packets, PLANE).transpose(1, 2, 0, 3)
    packets = packets.reshape(outer, rank + 16, plane_rows)
    scaled_plane = packets[0, :rank]
    labels_plane = packets[0, rank].astype(jnp.int32)

    blocks = []
    for by in range(outer):
        at = (level + by) % outer * piece
        block = lax.dynamic_slice_in_dim(act_plane, at, piece, 1)
        blocks.append(shifted(block, "z", by) if by else block)

    small = jobs * rank * outer * inner * rows <= 1 << 22
    half = inner * rows

    frozen = dot(act_plane, weight, 1, 0).reshape(groups, inner, rows, out_width)
    pairs = frozen.reshape(groups, inner // 2, 2, rows, out_width)
    kept = lax.dynamic_index_in_dim(pairs, place % 2, 2, keepdims=False)
    leaving = lax.dynamic_index_in_dim(pairs, 1 - place % 2, 2, keepdims=False)
    frozen = kept + swapped(leaving.astype(BF16), "q", 1).astype(F32)

    back = dot(upstream_plane, weight, 1, 1)
    reduced = jnp.zeros((rank, plane_rows), F32)
    turned_labels = labels_plane ^ place

    def step(carry, operands, keys=turned_labels, wanted=np.arange(inner)):
        back, reduced = carry
        block, first = operands
        keys = keys - first
        back = back + dot(spread(scaled_plane, keys, wanted), block, 0, 0)
        reduced = reduced + own_of(dot(block, act_plane, 1, 1), keys, wanted)
        return (back, reduced), None

    if small:
        turn = (level - turned_labels // inner) % outer * inner + turned_labels % inner
        (back, reduced), _ = step((back, reduced), (down_all, 0), turn, np.arange(jobs))
    else:
        firsts = (level - jnp.arange(outer, dtype=jnp.int32)) % outer * inner
        stack = (down_all.reshape(outer, inner * rank, flat), firsts)
        (back, reduced), _ = lax.scan(step, (back, reduced), stack)
    back = back.astype(BF16)

    reduced = reduced.reshape(rank, groups, inner * rows)
    total = lax.dynamic_index_in_dim(reduced, group, 1, keepdims=False)
    for by in range(1, groups):
        leaving = lax.dynamic_index_in_dim(reduced, (group + by) % groups, 1, keepdims=False)
        total = total + shifted(leaving, "groups", by)
    bit = inner // 2
    while bit:
        other = swapped(total, "q", bit)
        if bit == inner // 2:
            *blocks, packets, back, other = lax.optimization_barrier(
                (*blocks, packets, back, other)
            )
        total = total + other
        bit //= 2
    back = exchanged(back, PLANE)
    if aligned:
        turned = [(to, at, size) for at, to, size in moves]
        entering_derivative = repacked(back, (rows, width), turned)
    else:
        entering_derivative = back.reshape(groups, inner, rows, outer, piece)
        entering_derivative = entering_derivative.transpose(2, 3, 1, 0, 4).reshape(rows, width)
    reduced = total.astype(BF16)
    reduced_own = lax.dynamic_slice_in_dim(reduced, place * rows, rows, 1)

    upstream_group = lax.dynamic_slice_in_dim(upstream_plane, group * half, half, 0)
    labels_group = lax.dynamic_slice_in_dim(labels_plane, group * half, half, 0)
    wide = spread(reduced, labels_group - place, np.arange(outer) * inner)
    up_part = (ADAPTER_SCALE * dot(wide, upstream_group, 1, 0)).reshape(outer, rank, out_width)
    up_grad = lax.dynamic_index_in_dim(up_part, level, 0, keepdims=False)
    up_send = up_part.astype(BF16)
    *blocks, up_send = lax.optimization_barrier((*blocks, up_send))
    up_got = []
    for by in range(1, outer):
        leaving = lax.dynamic_index_in_dim(up_send, (level + by) % outer, 0, keepdims=False)
        up_got.append(shifted(leaving, "z", by))

    def down_grad_part(g, first, count):
        total = jnp.zeros((count * rank, piece), F32)
        for packet, block in zip(packets, blocks):
            packet = packet[:, g * half : (g + 1) * half]
            keys = packet[rank].astype(jnp.int32) - first
            wide = spread(packet[:rank], keys, np.arange(count))
            total = total + dot(wide, block[g * half : (g + 1) * half], 1, 0)
        return total.astype(BF16)

    if small:
        down_parts = [down_grad_part(g, 0, jobs) for g in range(groups)]
    else:
        down_parts = [
            lax.map(
                functools.partial(lambda g, b: down_grad_part(g, b * inner, inner), g),
                jnp.arange(outer, dtype=jnp.int32),
            ).reshape(jobs * rank, piece)
            for g in range(groups)
        ]
    down_parts = jnp.concatenate(down_parts, axis=0)
    down_parts, *up_got = lax.optimization_barrier((down_parts, *up_got))
    for got in up_got:
        up_grad = up_grad + got.astype(F32)

    bit = 2
    while bit < inner:
        pairs = frozen.reshape(groups, inner // bit // 2, 2, rows, out_width)
        mine = (place // bit) % 2
        kept = lax.dynamic_index_in_dim(pairs, mine, 2, keepdims=False)
        leaving = lax.dynamic_index_in_dim(pairs, 1 - mine, 2, keepdims=False)
        other = swapped(leaving.astype(BF16), "q", bit)
        if bit == 2:
            other, down_parts = lax.optimization_barrier((other, down_parts))
        frozen = kept + other.astype(F32)
        bit *= 2
    frozen = frozen.reshape(groups, rows, out_width)
    total = lax.dynamic_index_in_dim(frozen, group, 0, keepdims=False)
    for by in range(1, groups):
        leaving = lax.dynamic_index_in_dim(frozen, (group + by) % groups, 0, keepdims=False)
        total = total + shifted(leaving.astype(BF16), "groups", by).astype(F32)
    frozen = total

    down_parts = exchanged(down_parts, ("groups", "z", "q"))
    down_parts = down_parts.reshape(groups, outer, inner, rank, piece)
    down_grad = down_parts.transpose(3, 1, 2, 0, 4).reshape(rank, width).astype(F32).T
    wide = spread(reduced_own, row_job_labels, up_jobs)
    projected = (frozen + ADAPTER_SCALE * dot(wide, up_all, 0, 0)).astype(BF16)

    return (projected, entering_derivative, down_grad[None], up_grad[None])


def solution(mesh):
    groups, devices = mesh.devices.shape
    inner = 1
    while inner * inner < devices:
        inner *= 2
    fine = Mesh(
        mesh.devices.reshape(groups, devices // inner, inner), ("groups", "z", "q")
    )
    every = ("groups", "z", "q")
    owner = ("z", "q")
    return jax.shard_map(
        per_device,
        mesh=fine,
        in_specs=(
            P(every, None),
            P(every, None),
            P(every),
            P(owner, None),
            P(owner, None, None),
            P(owner, None, None),
        ),
        out_specs=(
            P(every, None),
            P(every, None),
            P(every, None, None),
            P(every, None, None),
        ),
        check_vma=False,
    )
```

```python
import functools

import jax
import jax.numpy as jnp
import numpy as np
from jax import lax
from jax.experimental import pallas as pl
from jax.experimental.pallas import tpu as pltpu
from jax.sharding import Mesh
from jax.sharding import PartitionSpec as P

ADAPTER_SCALE = 2.0
PLANE = ("groups", "q")
F32 = jnp.float32
BF16 = jnp.bfloat16


def swapped(array, axis, bit):
    peers = lax.axis_size(axis)
    return lax.ppermute(array, axis, [(i, i ^ bit) for i in range(peers)])


def shifted(array, axis, by):
    peers = lax.axis_size(axis)
    return lax.ppermute(array, axis, [(i, (i + by) % peers) for i in range(peers)])


def cube_gather(array, axes):
    stack = array[None]
    for axis in axes:
        bit = lax.axis_size(axis) // 2
        while bit:
            mine = (lax.axis_index(axis) & bit) > 0
            other = swapped(stack, axis, bit)
            pair = jnp.stack(
                [jnp.where(mine, other, stack), jnp.where(mine, stack, other)], axis=1
            )
            stack = pair.reshape((-1,) + array.shape)
            bit //= 2
    return stack


def relative(array, axis):
    return [array] + [shifted(array, axis, by) for by in range(1, lax.axis_size(axis))]


def placed(blocks, axis):
    me = lax.axis_index(axis)
    stack = jnp.zeros((len(blocks),) + blocks[0].shape, blocks[0].dtype)
    for by, block in enumerate(blocks):
        stack = lax.dynamic_update_index_in_dim(stack, block, (me - by) % len(blocks), 0)
    return stack


def repacked(array, shape, moves, kind=BF16):
    def kernel(source, target):
        for (r, c), (to_r, to_c), (high, wide) in moves:
            block = source[pl.ds(r, high), pl.ds(c, wide)]
            target[pl.ds(to_r, high), pl.ds(to_c, wide)] = block.astype(kind)

    return pl.pallas_call(
        kernel,
        out_shape=jax.ShapeDtypeStruct(shape, kind),
        in_specs=[pl.BlockSpec(memory_space=pltpu.VMEM)],
        out_specs=pl.BlockSpec(memory_space=pltpu.VMEM),
        compiler_params=pltpu.CompilerParams(vmem_limit_bytes=16 << 20),
        cost_estimate=pl.CostEstimate(
            flops=0, bytes_accessed=2 * array.size * array.dtype.itemsize, transcendentals=0
        ),
    )(array)


def exchanged(array, axes):
    return lax.all_to_all(array, axes, split_axis=0, concat_axis=0, tiled=True)


def after(values, *earlier):
    return lax.optimization_barrier((values, earlier))[0]


def dot(left, right, left_dim, right_dim):
    return lax.dot_general(
        left, right, (((left_dim,), (right_dim,)), ((), ())), preferred_element_type=F32
    )


def per_device(
    activations,
    upstream,
    row_job_labels,
    value_projection_weight,
    adapter_down_weight,
    adapter_up_weight,
):
    rows, width = activations.shape
    out_width = upstream.shape[1]
    rank = adapter_down_weight.shape[2]
    groups, outer, inner = (lax.axis_size(a) for a in ("groups", "z", "q"))
    group, level, place = (lax.axis_index(a) for a in ("groups", "z", "q"))
    plane = groups * inner
    jobs = outer * inner
    piece = width // (jobs * groups)
    flat = outer * piece
    plane_rows = plane * rows

    def spread(values, keys, wanted):
        hit = keys[None, None, :] == wanted.astype(np.int32)[:, None, None]
        wide = jnp.where(hit, values[None], jnp.zeros((), values.dtype))
        return wide.reshape(wanted.shape[0] * rank, -1)

    def own_of(wide, keys, wanted):
        hit = keys[None, None, :] == wanted.astype(np.int32)[:, None, None]
        wide = wide.reshape(wanted.shape[0], rank, -1)
        return jnp.sum(jnp.where(hit, wide, 0.0), axis=0)

    aligned = piece % 128 == 0 and rows % 16 == 0
    moves = []
    for g in range(groups):
        for p in range(inner):
            for o in range(outer):
                wide_at = (0, ((o * inner + p) * groups + g) * piece)
                flat_at = ((g * inner + p) * rows, o * piece)
                moves.append((wide_at, flat_at, (rows, piece)))

    if aligned:
        act_send = repacked(activations, (plane_rows, flat), moves)
    else:
        act_send = activations.reshape(rows, outer, inner, groups, piece)
        act_send = act_send.transpose(3, 2, 0, 1, 4).reshape(plane_rows, flat)
    part = value_projection_weight.shape[0] // groups
    weight_half = lax.dynamic_slice_in_dim(value_projection_weight, group * part, part, 0)
    if aligned and rank % 16 == 0:

        def pick(which, source, target):
            for p in range(inner):
                for o in range(outer):
                    at = pl.multiple_of(((o * inner + p) * groups + which[0]) * piece, 128)
                    target[pl.ds(p * rank, rank), pl.ds(o * piece, piece)] = source[
                        :, pl.ds(at, piece)
                    ]

        down_send = pl.pallas_call(
            pick,
            out_shape=jax.ShapeDtypeStruct((inner * rank, flat), BF16),
            in_specs=[
                pl.BlockSpec(memory_space=pltpu.SMEM),
                pl.BlockSpec(memory_space=pltpu.VMEM),
            ],
            out_specs=pl.BlockSpec(memory_space=pltpu.VMEM),
            compiler_params=pltpu.CompilerParams(vmem_limit_bytes=16 << 20),
            cost_estimate=pl.CostEstimate(
                flops=0, bytes_accessed=3 * rank * width, transcendentals=0
            ),
        )(group.astype(jnp.int32)[None], adapter_down_weight[0].T)
        down_send = down_send.reshape(inner, rank, flat)
    else:
        down_send = adapter_down_weight[0].T.reshape(rank, outer, inner, groups, piece)
        down_send = lax.dynamic_index_in_dim(down_send, group, 3, keepdims=False)
        down_send = down_send.transpose(2, 0, 1, 3).reshape(inner, rank, flat)
    down_block = []
    for other in range(inner):
        leaving = lax.dynamic_index_in_dim(down_send, place ^ other, 0, keepdims=False)
        down_block.append(swapped(leaving, "q", other) if other else leaving)
    down_block = jnp.concatenate(down_block, axis=0).reshape(-1, out_width)

    both = jnp.concatenate([weight_half, down_block], axis=0)

    up_own, *up_others = relative(adapter_up_weight[0], "z")
    both, act_send, *up_others = lax.optimization_barrier((both, act_send, *up_others))
    up_all = placed([up_own, *up_others], "z").reshape(1, outer * rank, out_width)
    up_other = swapped(up_all, "q", inner // 2)
    up_jobs = (np.arange(outer)[None, :] * inner + np.arange(inner)[:, None]).reshape(-1)
    act_plane = exchanged(act_send, PLANE)

    shares = {0: (weight_half, down_block)}
    rising, falling = shifted(both, "z", by=1), shifted(both, "z", by=-1)
    act_plane, rising, falling, upstream, up_other = lax.optimization_barrier(
        (act_plane, rising, falling, upstream, up_other)
    )
    for by in range(1, outer // 2):
        if by > 1:
            rising, falling = shifted(rising, "z", by=1), shifted(falling, "z", by=-1)
        shares[by] = rising[:part], rising[part:]
        shares[outer - by] = falling[:part], falling[part:]
    shares[outer // 2] = shifted(rising[:part], "z", by=1), shifted(falling[part:], "z", by=-1)

    bit = inner // 2
    while bit:
        mine = (place & bit) > 0
        other = up_other if bit == inner // 2 else swapped(up_all, "q", bit)
        pair = [jnp.where(mine, other, up_all), jnp.where(mine, up_all, other)]
        up_all = jnp.stack(pair, axis=1).reshape(-1, outer * rank, out_width)
        bit //= 2
    up_all = up_all.reshape(jobs * rank, out_width)

    wide = ADAPTER_SCALE * dot(up_all, upstream, 1, 1)
    scaled = own_of(wide, row_job_labels, up_jobs).astype(BF16)
    label_rows = jnp.broadcast_to(row_job_labels.astype(BF16)[None], (16, rows))
    packet = jnp.concatenate([scaled, label_rows], axis=0)
    act_plane, packet, upstream = lax.optimization_barrier((act_plane, packet, upstream))
    shares[outer // 2] = after(shares[outer // 2], packet)
    packets = jnp.stack(relative(packet, "z"))

    weight = placed([shares[by][0] for by in range(outer)], "z").reshape(flat, out_width)
    down_all = jnp.concatenate([shares[by][1] for by in range(outer)], axis=0)
    down_all = down_all.reshape(jobs * rank, flat)

    upstream_plane = cube_gather(upstream, PLANE).reshape(plane_rows, out_width)
    packets = cube_gather(packets, PLANE).transpose(1, 2, 0, 3)
    packets = packets.reshape(outer, rank + 16, plane_rows)
    scaled_plane = packets[0, :rank]
    labels_plane = packets[0, rank].astype(jnp.int32)

    blocks = []
    for by in range(outer):
        at = (level + by) % outer * piece
        block = lax.dynamic_slice_in_dim(act_plane, at, piece, 1)
        blocks.append(shifted(block, "z", by) if by else block)

    small = jobs * rank * outer * inner * rows <= 1 << 22
    half = inner * rows

    frozen = dot(act_plane, weight, 1, 0).reshape(groups, inner, rows, out_width)
    pairs = frozen.reshape(groups, inner // 2, 2, rows, out_width)
    kept = lax.dynamic_index_in_dim(pairs, place % 2, 2, keepdims=False)
    leaving = lax.dynamic_index_in_dim(pairs, 1 - place % 2, 2, keepdims=False)
    frozen = kept + swapped(leaving.astype(BF16), "q", 1).astype(F32)

    back = dot(upstream_plane, weight, 1, 1)
    reduced = jnp.zeros((rank, plane_rows), F32)
    turned_labels = labels_plane ^ place

    def step(carry, operands, keys=turned_labels, wanted=np.arange(inner)):
        back, reduced = carry
        block, first = operands
        keys = keys - first
        back = back + dot(spread(scaled_plane, keys, wanted), block, 0, 0)
        reduced = reduced + own_of(dot(block, act_plane, 1, 1), keys, wanted)
        return (back, reduced), None

    if small:
        turn = (level - turned_labels // inner) % outer * inner + turned_labels % inner
        (back, reduced), _ = step((back, reduced), (down_all, 0), turn, np.arange(jobs))
    else:
        firsts = (level - jnp.arange(outer, dtype=jnp.int32)) % outer * inner
        stack = (down_all.reshape(outer, inner * rank, flat), firsts)
        (back, reduced), _ = lax.scan(step, (back, reduced), stack)
    back = back.astype(BF16)

    reduced = reduced.reshape(rank, groups, inner * rows)
    total = lax.dynamic_index_in_dim(reduced, group, 1, keepdims=False)
    for by in range(1, groups):
        leaving = lax.dynamic_index_in_dim(reduced, (group + by) % groups, 1, keepdims=False)
        total = total + shifted(leaving, "groups", by)
    bit = inner // 2
    while bit:
        other = swapped(total, "q", bit)
        if bit == inner // 2:
            packets = after(packets, back)
            back = after(back, other)
        total = total + other
        bit //= 2
    back = exchanged(back, PLANE)
    if aligned:
        turned = [(to, at, size) for at, to, size in moves]
        entering_derivative = repacked(back, (rows, width), turned)
    else:
        entering_derivative = back.reshape(groups, inner, rows, outer, piece)
        entering_derivative = entering_derivative.transpose(2, 3, 1, 0, 4).reshape(rows, width)
    reduced = total.astype(BF16)
    reduced_own = lax.dynamic_slice_in_dim(reduced, place * rows, rows, 1)

    upstream_group = lax.dynamic_slice_in_dim(upstream_plane, group * half, half, 0)
    labels_group = lax.dynamic_slice_in_dim(labels_plane, group * half, half, 0)
    wide = spread(reduced, labels_group - place, np.arange(outer) * inner)
    up_part = (ADAPTER_SCALE * dot(wide, upstream_group, 1, 0)).reshape(outer, rank, out_width)
    up_grad = lax.dynamic_index_in_dim(up_part, level, 0, keepdims=False)
    up_send = up_part.astype(BF16)
    packets = after(packets, up_send)
    up_got = []
    for by in range(1, outer):
        leaving = lax.dynamic_index_in_dim(up_send, (level + by) % outer, 0, keepdims=False)
        up_got.append(shifted(leaving, "z", by))

    def down_grad_part(g, first, count):
        total = jnp.zeros((count * rank, piece), F32)
        for packet, block in zip(packets, blocks):
            packet = packet[:, g * half : (g + 1) * half]
            keys = packet[rank].astype(jnp.int32) - first
            wide = spread(packet[:rank], keys, np.arange(count))
            total = total + dot(wide, block[g * half : (g + 1) * half], 1, 0)
        return total.astype(BF16)

    if small:
        down_parts = [down_grad_part(g, 0, jobs) for g in range(groups)]
    else:
        down_parts = [
            lax.map(
                functools.partial(lambda g, b: down_grad_part(g, b * inner, inner), g),
                jnp.arange(outer, dtype=jnp.int32),
            ).reshape(jobs * rank, piece)
            for g in range(groups)
        ]
    down_parts = jnp.concatenate(down_parts, axis=0)
    down_parts = after(down_parts, up_got, back)
    for got in up_got:
        up_grad = up_grad + got.astype(F32)

    bit = 2
    while bit < inner:
        pairs = frozen.reshape(groups, inner // bit // 2, 2, rows, out_width)
        mine = (place // bit) % 2
        kept = lax.dynamic_index_in_dim(pairs, mine, 2, keepdims=False)
        leaving = lax.dynamic_index_in_dim(pairs, 1 - mine, 2, keepdims=False)
        other = swapped(leaving.astype(BF16), "q", bit)
        if bit == 2:
            other, down_parts = lax.optimization_barrier((other, down_parts))
        frozen = kept + other.astype(F32)
        bit *= 2
    frozen = frozen.reshape(groups, rows, out_width)
    total = lax.dynamic_index_in_dim(frozen, group, 0, keepdims=False)
    for by in range(1, groups):
        leaving = lax.dynamic_index_in_dim(frozen, (group + by) % groups, 0, keepdims=False)
        total = total + shifted(leaving.astype(BF16), "groups", by).astype(F32)
    frozen = total

    down_parts = exchanged(down_parts, ("groups", "z", "q"))
    if aligned and rank % 16 == 0:
        homes = []
        for g in range(groups):
            for j in range(jobs):
                at = ((g * jobs + j) * rank, 0)
                homes.append((at, (0, (j * groups + g) * piece), (rank, piece)))
        down_grad = repacked(down_parts, (rank, width), homes, F32).T
    else:
        down_parts = down_parts.reshape(groups, outer, inner, rank, piece)
        down_grad = down_parts.transpose(3, 1, 2, 0, 4).reshape(rank, width).astype(F32).T

    wide = spread(reduced_own, row_job_labels, up_jobs)
    projected = (frozen + ADAPTER_SCALE * dot(wide, up_all, 0, 0)).astype(BF16)

    return (projected, entering_derivative, down_grad[None], up_grad[None])


def solution(mesh):
    groups, devices = mesh.devices.shape
    inner = 1
    while inner * inner < devices:
        inner *= 2
    fine = Mesh(
        mesh.devices.reshape(groups, devices // inner, inner), ("groups", "z", "q")
    )
    every = ("groups", "z", "q")
    owner = ("z", "q")
    return jax.shard_map(
        per_device,
        mesh=fine,
        in_specs=(
            P(every, None),
            P(every, None),
            P(every),
            P(owner, None),
            P(owner, None, None),
            P(owner, None, None),
        ),
        out_specs=(
            P(every, None),
            P(every, None),
            P(every, None, None),
            P(every, None, None),
        ),
        check_vma=False,
    )
```

```python
import functools

import jax
import jax.numpy as jnp
import numpy as np
from jax import lax
from jax.experimental import pallas as pl
from jax.experimental.pallas import tpu as pltpu
from jax.sharding import Mesh
from jax.sharding import PartitionSpec as P

ADAPTER_SCALE = 2.0
PLANE = ("groups", "q")
F32 = jnp.float32
BF16 = jnp.bfloat16


def swapped(array, axis, bit):
    peers = lax.axis_size(axis)
    return lax.ppermute(array, axis, [(i, i ^ bit) for i in range(peers)])


def shifted(array, axis, by):
    peers = lax.axis_size(axis)
    return lax.ppermute(array, axis, [(i, (i + by) % peers) for i in range(peers)])


def cube_gather(array, axes):
    stack = array[None]
    for axis in axes:
        bit = lax.axis_size(axis) // 2
        while bit:
            mine = (lax.axis_index(axis) & bit) > 0
            other = swapped(stack, axis, bit)
            pair = jnp.stack(
                [jnp.where(mine, other, stack), jnp.where(mine, stack, other)], axis=1
            )
            stack = pair.reshape((-1,) + array.shape)
            bit //= 2
    return stack


def relative(array, axis):
    return [array] + [shifted(array, axis, by) for by in range(1, lax.axis_size(axis))]


def placed(blocks, axis):
    me = lax.axis_index(axis)
    stack = jnp.zeros((len(blocks),) + blocks[0].shape, blocks[0].dtype)
    for by, block in enumerate(blocks):
        stack = lax.dynamic_update_index_in_dim(stack, block, (me - by) % len(blocks), 0)
    return stack


def repacked(array, shape, moves, kind=BF16):
    def kernel(source, target):
        for (r, c), (to_r, to_c), (high, wide) in moves:
            block = source[pl.ds(r, high), pl.ds(c, wide)]
            target[pl.ds(to_r, high), pl.ds(to_c, wide)] = block.astype(kind)

    return pl.pallas_call(
        kernel,
        out_shape=jax.ShapeDtypeStruct(shape, kind),
        in_specs=[pl.BlockSpec(memory_space=pltpu.VMEM)],
        out_specs=pl.BlockSpec(memory_space=pltpu.VMEM),
        compiler_params=pltpu.CompilerParams(vmem_limit_bytes=16 << 20),
        cost_estimate=pl.CostEstimate(
            flops=0, bytes_accessed=2 * array.size * array.dtype.itemsize, transcendentals=0
        ),
    )(array)


def exchanged(array, axes):
    return lax.all_to_all(array, axes, split_axis=0, concat_axis=0, tiled=True)


def after(values, *earlier):
    return lax.optimization_barrier((values, earlier))[0]


def dot(left, right, left_dim, right_dim):
    return lax.dot_general(
        left, right, (((left_dim,), (right_dim,)), ((), ())), preferred_element_type=F32
    )


def per_device(
    activations,
    upstream,
    row_job_labels,
    value_projection_weight,
    adapter_down_weight,
    adapter_up_weight,
):
    rows, width = activations.shape
    out_width = upstream.shape[1]
    rank = adapter_down_weight.shape[2]
    groups, outer, inner = (lax.axis_size(a) for a in ("groups", "z", "q"))
    group, level, place = (lax.axis_index(a) for a in ("groups", "z", "q"))
    plane = groups * inner
    jobs = outer * inner
    piece = width // (jobs * groups)
    flat = outer * piece
    plane_rows = plane * rows

    def spread(values, keys, wanted):
        hit = keys[None, None, :] == wanted.astype(np.int32)[:, None, None]
        wide = jnp.where(hit, values[None], jnp.zeros((), values.dtype))
        return wide.reshape(wanted.shape[0] * rank, -1)

    def own_of(wide, keys, wanted):
        hit = keys[None, None, :] == wanted.astype(np.int32)[:, None, None]
        wide = wide.reshape(wanted.shape[0], rank, -1)
        return jnp.sum(jnp.where(hit, wide, 0.0), axis=0)

    aligned = piece % 128 == 0 and rows % 16 == 0
    moves = []
    for g in range(groups):
        for p in range(inner):
            for o in range(outer):
                wide_at = (0, ((o * inner + p) * groups + g) * piece)
                flat_at = ((g * inner + p) * rows, o * piece)
                moves.append((wide_at, flat_at, (rows, piece)))

    if aligned:
        act_send = repacked(activations, (plane_rows, flat), moves)
    else:
        act_send = activations.reshape(rows, outer, inner, groups, piece)
        act_send = act_send.transpose(3, 2, 0, 1, 4).reshape(plane_rows, flat)
    part = value_projection_weight.shape[0] // groups
    weight_half = lax.dynamic_slice_in_dim(value_projection_weight, group * part, part, 0)
    if aligned and rank % 16 == 0:

        def pick(which, source, target):
            for p in range(inner):
                for o in range(outer):
                    at = pl.multiple_of(((o * inner + p) * groups + which[0]) * piece, 128)
                    target[pl.ds(p * rank, rank), pl.ds(o * piece, piece)] = source[
                        :, pl.ds(at, piece)
                    ]

        down_send = pl.pallas_call(
            pick,
            out_shape=jax.ShapeDtypeStruct((inner * rank, flat), BF16),
            in_specs=[
                pl.BlockSpec(memory_space=pltpu.SMEM),
                pl.BlockSpec(memory_space=pltpu.VMEM),
            ],
            out_specs=pl.BlockSpec(memory_space=pltpu.VMEM),
            compiler_params=pltpu.CompilerParams(vmem_limit_bytes=16 << 20),
            cost_estimate=pl.CostEstimate(
                flops=0, bytes_accessed=3 * rank * width, transcendentals=0
            ),
        )(group.astype(jnp.int32)[None], adapter_down_weight[0].T)
        down_send = down_send.reshape(inner, rank, flat)
    else:
        down_send = adapter_down_weight[0].T.reshape(rank, outer, inner, groups, piece)
        down_send = lax.dynamic_index_in_dim(down_send, group, 3, keepdims=False)
        down_send = down_send.transpose(2, 0, 1, 3).reshape(inner, rank, flat)
    down_block = []
    for other in range(inner):
        leaving = lax.dynamic_index_in_dim(down_send, place ^ other, 0, keepdims=False)
        down_block.append(swapped(leaving, "q", other) if other else leaving)
    down_block = jnp.concatenate(down_block, axis=0).reshape(-1, out_width)

    both = jnp.concatenate([weight_half, down_block], axis=0)

    up_own, *up_others = relative(adapter_up_weight[0], "z")
    both, act_send, *up_others = lax.optimization_barrier((both, act_send, *up_others))
    up_all = placed([up_own, *up_others], "z").reshape(1, outer * rank, out_width)
    up_other = swapped(up_all, "q", inner // 2)
    up_jobs = (np.arange(outer)[None, :] * inner + np.arange(inner)[:, None]).reshape(-1)
    act_plane = exchanged(act_send, PLANE)

    shares = {0: (weight_half, down_block)}
    rising, falling = shifted(both, "z", by=1), shifted(both, "z", by=-1)
    act_plane, rising, falling, upstream, up_other = lax.optimization_barrier(
        (act_plane, rising, falling, upstream, up_other)
    )
    for by in range(1, outer // 2):
        if by > 1:
            rising, falling = shifted(rising, "z", by=1), shifted(falling, "z", by=-1)
        shares[by] = rising[:part], rising[part:]
        shares[outer - by] = falling[:part], falling[part:]
    shares[outer // 2] = shifted(rising[:part], "z", by=1), shifted(falling[part:], "z", by=-1)

    bit = inner // 2
    while bit:
        mine = (place & bit) > 0
        other = up_other if bit == inner // 2 else swapped(up_all, "q", bit)
        pair = [jnp.where(mine, other, up_all), jnp.where(mine, up_all, other)]
        up_all = jnp.stack(pair, axis=1).reshape(-1, outer * rank, out_width)
        bit //= 2
    up_all = up_all.reshape(jobs * rank, out_width)

    wide = ADAPTER_SCALE * dot(up_all, upstream, 1, 1)
    scaled = own_of(wide, row_job_labels, up_jobs).astype(BF16)
    label_rows = jnp.broadcast_to(row_job_labels.astype(BF16)[None], (16, rows))
    packet = jnp.concatenate([scaled, label_rows], axis=0)
    act_plane, packet, upstream = lax.optimization_barrier((act_plane, packet, upstream))
    packets = jnp.stack(relative(packet, "z"))

    weight = placed([shares[by][0] for by in range(outer)], "z").reshape(flat, out_width)
    down_all = jnp.concatenate([shares[by][1] for by in range(outer)], axis=0)
    down_all = down_all.reshape(jobs * rank, flat)

    upstream_plane = cube_gather(upstream, PLANE).reshape(plane_rows, out_width)
    packets = cube_gather(packets, PLANE).transpose(1, 2, 0, 3)
    packets = packets.reshape(outer, rank + 16, plane_rows)
    scaled_plane = packets[0, :rank]
    labels_plane = packets[0, rank].astype(jnp.int32)

    blocks = []
    for by in range(outer):
        at = (level + by) % outer * piece
        block = lax.dynamic_slice_in_dim(act_plane, at, piece, 1)
        blocks.append(shifted(block, "z", by) if by else block)

    small = jobs * rank * outer * inner * rows <= 1 << 22
    half = inner * rows

    frozen = dot(act_plane, weight, 1, 0).reshape(groups, inner, rows, out_width)
    pairs = frozen.reshape(groups, inner // 2, 2, rows, out_width)
    kept = lax.dynamic_index_in_dim(pairs, place % 2, 2, keepdims=False)
    leaving = lax.dynamic_index_in_dim(pairs, 1 - place % 2, 2, keepdims=False)
    frozen = kept + swapped(leaving.astype(BF16), "q", 1).astype(F32)

    back = dot(upstream_plane, weight, 1, 1)
    reduced = jnp.zeros((rank, plane_rows), F32)
    turned_labels = labels_plane ^ place

    def step(carry, operands, keys=turned_labels, wanted=np.arange(inner)):
        back, reduced = carry
        block, first = operands
        keys = keys - first
        back = back + dot(spread(scaled_plane, keys, wanted), block, 0, 0)
        reduced = reduced + own_of(dot(block, act_plane, 1, 1), keys, wanted)
        return (back, reduced), None

    if small:
        turn = (level - turned_labels // inner) % outer * inner + turned_labels % inner
        (back, reduced), _ = step((back, reduced), (down_all, 0), turn, np.arange(jobs))
    else:
        firsts = (level - jnp.arange(outer, dtype=jnp.int32)) % outer * inner
        stack = (down_all.reshape(outer, inner * rank, flat), firsts)
        (back, reduced), _ = lax.scan(step, (back, reduced), stack)
    back = back.astype(BF16)

    reduced = reduced.reshape(rank, groups, inner * rows)
    total = lax.dynamic_index_in_dim(reduced, group, 1, keepdims=False)
    for by in range(1, groups):
        leaving = lax.dynamic_index_in_dim(reduced, (group + by) % groups, 1, keepdims=False)
        total = total + shifted(leaving, "groups", by)
    bit = inner // 2
    while bit:
        other = swapped(total, "q", bit)
        if bit == inner // 2:
            packets = after(packets, back)
            back = after(back, other)
        total = total + other
        bit //= 2
    back = exchanged(back, PLANE)
    if aligned:
        turned = [(to, at, size) for at, to, size in moves]
        entering_derivative = repacked(back, (rows, width), turned)
    else:
        entering_derivative = back.reshape(groups, inner, rows, outer, piece)
        entering_derivative = entering_derivative.transpose(2, 3, 1, 0, 4).reshape(rows, width)
    reduced = total.astype(BF16)
    reduced_own = lax.dynamic_slice_in_dim(reduced, place * rows, rows, 1)

    upstream_group = lax.dynamic_slice_in_dim(upstream_plane, group * half, half, 0)
    labels_group = lax.dynamic_slice_in_dim(labels_plane, group * half, half, 0)
    wide = spread(reduced, labels_group - place, np.arange(outer) * inner)
    up_part = (ADAPTER_SCALE * dot(wide, upstream_group, 1, 0)).reshape(outer, rank, out_width)
    up_grad = lax.dynamic_index_in_dim(up_part, level, 0, keepdims=False)
    up_send = up_part.astype(BF16)
    packets = after(packets, up_send)
    up_got = []
    for by in range(1, outer):
        leaving = lax.dynamic_index_in_dim(up_send, (level + by) % outer, 0, keepdims=False)
        up_got.append(shifted(leaving, "z", by))

    def down_grad_part(g, first, count):
        total = jnp.zeros((count * rank, piece), F32)
        for packet, block in zip(packets, blocks):
            packet = packet[:, g * half : (g + 1) * half]
            keys = packet[rank].astype(jnp.int32) - first
            wide = spread(packet[:rank], keys, np.arange(count))
            total = total + dot(wide, block[g * half : (g + 1) * half], 1, 0)
        return total.astype(BF16)

    if small:
        down_parts = [down_grad_part(g, 0, jobs) for g in range(groups)]
    else:
        down_parts = [
            lax.map(
                functools.partial(lambda g, b: down_grad_part(g, b * inner, inner), g),
                jnp.arange(outer, dtype=jnp.int32),
            ).reshape(jobs * rank, piece)
            for g in range(groups)
        ]
    down_parts = jnp.concatenate(down_parts, axis=0)
    down_parts = after(down_parts, up_got, back)
    for got in up_got:
        up_grad = up_grad + got.astype(F32)

    bit = 2
    while bit < inner:
        pairs = frozen.reshape(groups, inner // bit // 2, 2, rows, out_width)
        mine = (place // bit) % 2
        kept = lax.dynamic_index_in_dim(pairs, mine, 2, keepdims=False)
        leaving = lax.dynamic_index_in_dim(pairs, 1 - mine, 2, keepdims=False)
        other = swapped(leaving.astype(BF16), "q", bit)
        if bit == 2:
            other, down_parts = lax.optimization_barrier((other, down_parts))
        frozen = kept + other.astype(F32)
        bit *= 2
    frozen = frozen.reshape(groups, rows, out_width)
    total = lax.dynamic_index_in_dim(frozen, group, 0, keepdims=False)
    for by in range(1, groups):
        leaving = lax.dynamic_index_in_dim(frozen, (group + by) % groups, 0, keepdims=False)
        total = total + shifted(leaving.astype(BF16), "groups", by).astype(F32)
    frozen = total

    down_parts = exchanged(down_parts, ("groups", "z", "q"))
    if aligned and rank % 16 == 0:
        homes = []
        for g in range(groups):
            for j in range(jobs):
                at = ((g * jobs + j) * rank, 0)
                homes.append((at, (0, (j * groups + g) * piece), (rank, piece)))
        down_grad = repacked(down_parts, (rank, width), homes, F32).T
    else:
        down_parts = down_parts.reshape(groups, outer, inner, rank, piece)
        down_grad = down_parts.transpose(3, 1, 2, 0, 4).reshape(rank, width).astype(F32).T

    wide = spread(reduced_own, row_job_labels, up_jobs)
    projected = (frozen + ADAPTER_SCALE * dot(wide, up_all, 0, 0)).astype(BF16)

    return (projected, entering_derivative, down_grad[None], up_grad[None])


def solution(mesh):
    groups, devices = mesh.devices.shape
    inner = 1
    while inner * inner < devices:
        inner *= 2
    fine = Mesh(
        mesh.devices.reshape(groups, devices // inner, inner), ("groups", "z", "q")
    )
    every = ("groups", "z", "q")
    owner = ("z", "q")
    return jax.shard_map(
        per_device,
        mesh=fine,
        in_specs=(
            P(every, None),
            P(every, None),
            P(every),
            P(owner, None),
            P(owner, None, None),
            P(owner, None, None),
        ),
        out_specs=(
            P(every, None),
            P(every, None),
            P(every, None, None),
            P(every, None, None),
        ),
        check_vma=False,
    )
```
